32 devices in a mesh: dp: 4 (over z), seq: 8 (over y, x, core).
Axes of the slice: x: 2, y: 2, z: 4, core: 2. Of those that a mesh axis runs over, the one named last changes fastest.
Arguments:
- tokens: bfloat16 [1024, 2880], P('seq', 'dp'), may hold values from -6 to 6
- upstream: bfloat16 [1024, 2880], P('seq', 'dp'), may hold values from -6 to 6
- norm_gain: bfloat16 [2880], replicated, may hold values from 0.5 to 1.5
- experts: int32 [1024, 4], P('seq'), may hold values from 0 to 15, all different within a row; in each aligned block of 128 rows (0 to 127, 128 to 255, ...) at most 48 rows name the same one
- route_weights: bfloat16 [1024, 4], P('seq'), may hold values from 0.049804688 to 0.59765625
- w_gate_up: bfloat16 [16, 2880, 2, 1440], P('seq', None, None, 'dp'), may hold values from -0.109375 to 0.109375
- w_down: bfloat16 [16, 1440, 2880], P('seq', 'dp'), may hold values from -0.15625 to 0.15625
Outputs:
- token_gradient: bfloat16 [1024, 2880], P('seq', 'dp')
- gain_gradient: float32 [2880], P('dp')
- grad_weights: float32 [1024, 4], P('seq')
- grad_gate_up: bfloat16 [16, 2880, 2, 1440], P('seq', None, None, 'dp')
- grad_down: bfloat16 [16, 1440, 2880], P('seq', 'dp')
The draws below stay inside these ranges and needn't reach their ends.
Inputs may be any that keep to these rules, and one draw needn't show every extreme that they name: Each row names 4 different experts. In each aligned block of 128 rows (the tokens of one index of seq) no expert is named more than 48 times, a bound that some block reaches.
All inputs are finite; a program needn't handle non-finite values.
Results may differ from the reference program's by a relative error of at most 0.012.
Values may be sent and summed in bfloat16 or wider, within the bound.
A program may use at most 128 MiB of HBM per device.

```python
import math
import jax
import jax.numpy as jnp
import numpy as np
from jax import lax

MODEL_WIDTH = 2880
FF = 1440
TOP = 4
TOK_DEV = 128
EXPERTS = 16
TOKENS = 1024
CAP = 48
N_SEQ = 8


def steps_of(rng, shape, shards, smallest, high):
    factor_of, own = 1.0, jax.random.fold_in(rng, 6)
    for axis_at, shards_of in shards:
        heights = jnp.exp(jax.random.uniform(jax.random.fold_in(own, axis_at), (shards_of,), jnp.float32, smallest / len(shards), high / len(shards)))
        factor_of = factor_of * jnp.repeat(heights, shape[axis_at] // shards_of).reshape([-1 if axis == axis_at else 1 for axis in range(len(shape))])
    return factor_of


def routed_block(stream_key, own, number, rows, number_of, top, bound, slope):
    sequence = jax.random.permutation(stream_key, number_of)
    heavy_load, usual = portions_of(number_of, rows * top, bound, slope, True), portions_of(number_of, rows * top, bound, slope, False)
    places = jnp.arange(number_of)

    def named(lengths, offset_by):
        used = int((lengths > 0).sum())
        fixed = max(1, used // 4)
        moved = fixed + (places - fixed + offset_by * (used - fixed)) % max(1, number_of - fixed)
        return jnp.zeros((number_of,), jnp.int32).at[sequence[jnp.where(places < fixed, places, moved)]].set(jnp.asarray(lengths, jnp.int32))

    lengths = jnp.where(number % 4 == 0, named(heavy_load, number // 4), named(usual, number - number // 4 - 1))
    mixed = jax.random.permutation(jax.random.fold_in(own, 3), number_of)
    source_of, sink = mixed[0:number_of // 2 * 2:2], mixed[1:number_of // 2 * 2:2]
    slack = jnp.minimum(lengths[source_of] - 1, bound - lengths[sink]) // 2
    slack = jnp.where((source_of == sequence[0]) | (sink == sequence[0]) | (lengths[sink] == 0), 0, jnp.maximum(slack, 0))
    moved = jax.random.randint(jax.random.fold_in(own, 4), (number_of // 2,), 0, 1 << 20) % (slack + 1)
    lengths = lengths.at[source_of].add(-moved).at[sink].add(moved)
    labels = jnp.searchsorted(jnp.cumsum(lengths), jnp.arange(rows * top), side="right").astype(jnp.int32)
    listing = labels.reshape(top, rows).T
    listing = listing[jax.random.permutation(jax.random.fold_in(own, 1), rows)]
    offset_by = jax.random.randint(jax.random.fold_in(own, 2), (rows, 1), 0, top)
    return jnp.take_along_axis(listing, (jnp.arange(top)[None, :] + offset_by) % top, axis=1)


def portions_of(number_of, total, most, lean, full):
    portions = [(1 << 20) // math.isqrt(standing ** lean) + 1 for standing in range(1, number_of + 1)]
    largest = most if full else min(most, max(-(-total // number_of), total * portions[0] // sum(portions)))
    least = 1 if total - largest >= number_of - 1 else 0
    counts, rest = [largest] + [least] * (number_of - 1), total - largest - least * (number_of - 1)
    while rest > 0:
        candidates = [i for i in range(1, number_of) if counts[i] < largest] or [i for i in range(1, number_of) if counts[i] < most]
        whole, left = sum([portions[i] for i in candidates]), rest
        for i in candidates:
            addition = min(most - counts[i], max(1, left * portions[i] // whole), rest)
            counts[i] = counts[i] + addition
            rest = rest - addition
    return np.array(counts)


def gaussian(stream_key, extent, scale, reach, split=(), kind=jnp.bfloat16):
    array = jax.random.normal(stream_key, extent, jnp.float32) * scale
    if len(split) > 0:
        array = steps_of(stream_key, extent, split, -0.22, 0.18) * array
    return jnp.clip(array, min=-reach, max=reach).astype(kind)


def setup_inputs(seed: int = 0) -> dict:
    streams_of = jax.random.split(jax.random.key(seed), 8)
    tokens = gaussian(streams_of[0], (TOKENS, MODEL_WIDTH), 1.0, 6.0, ((0, 8), (1, 4)))
    upstream = gaussian(streams_of[1], (TOKENS, MODEL_WIDTH), 1.0, 6.0, ((0, 8), (1, 4)))
    norm_gain = jnp.clip(1.0 + 0.1 * jax.random.normal(streams_of[2], (MODEL_WIDTH,), jnp.float32), 0.5, 1.5).astype(jnp.bfloat16)
    experts_keys = jax.random.split(jax.random.fold_in(streams_of[3], 1), TOKENS // TOK_DEV)
    experts_turns = jax.random.permutation(jax.random.fold_in(streams_of[3], 3), TOKENS // TOK_DEV)
    experts = jax.vmap(lambda own, number: routed_block(jax.random.fold_in(streams_of[3], 2), own, number, TOK_DEV, EXPERTS, TOP, CAP, 2))(experts_keys, experts_turns).reshape((TOKENS, TOP))
    route_weights = jnp.clip(0.049804688 + 0.54785156 * jax.random.uniform(streams_of[4], (TOKENS, TOP), jnp.float32) ** steps_of(streams_of[4], (TOKENS, TOP), ((0, 8),), -0.2, 0.2), 0.049804688, 0.59765625).astype(jnp.bfloat16)
    w_gate_up = gaussian(streams_of[5], (EXPERTS, MODEL_WIDTH, 2, FF), MODEL_WIDTH ** -0.5, 0.109375, ((0, 8), (3, 4)))
    w_down = gaussian(streams_of[6], (EXPERTS, FF, MODEL_WIDTH), FF ** -0.5, 0.15625, ((0, 8), (1, 4)))
    return {"tokens": tokens, "upstream": upstream, "norm_gain": norm_gain, "experts": experts, "route_weights": route_weights, "w_gate_up": w_gate_up, "w_down": w_down}


def expert_terms(x_rows, dy_rows, weight_rows, w_gu, w_dn):
    width = x_rows.shape[1]
    hidden = w_dn.shape[0]
    flat_gu = w_gu.reshape(width, 2 * hidden)
    projected = jnp.dot(x_rows, flat_gu, preferred_element_type=jnp.float32)
    gate_pre = projected[:, :hidden]
    up_pre = projected[:, hidden:]
    sig_gate = jax.nn.sigmoid(1.702 * gate_pre)
    glu_value = gate_pre * sig_gate
    activated = ((up_pre + 1.0) * glu_value).astype(jnp.bfloat16)
    back_proj = lax.dot_general(dy_rows, w_dn, (((1,), (1,)), ((), ())), preferred_element_type=jnp.float32)
    row_weight = weight_rows.astype(jnp.float32)[:, None]
    weight_grad = lax.optimization_barrier(jnp.sum(activated.astype(jnp.float32) * back_proj, axis=1))
    dact = row_weight * back_proj
    dgate_pre = dact * (up_pre + 1.0) * (sig_gate + 1.702 * gate_pre * sig_gate * (1.0 - sig_gate))
    dup_pre = dact * glu_value
    dproj = jnp.concatenate([dgate_pre, dup_pre], axis=1).astype(jnp.bfloat16)
    scaled = (row_weight * activated.astype(jnp.float32)).astype(jnp.bfloat16)
    grad_dn = lax.dot_general(scaled, dy_rows, (((0,), (0,)), ((), ())), preferred_element_type=jnp.float32)
    grad_gu = lax.dot_general(x_rows, dproj, (((0,), (0,)), ((), ())), preferred_element_type=jnp.float32)
    grad_rows = lax.dot_general(dproj, flat_gu, (((1,), (1,)), ((), ())), preferred_element_type=jnp.float32)
    return (grad_gu, grad_dn, grad_rows, weight_grad)

def reference(tokens, upstream, norm_gain, experts, route_weights, w_gate_up, w_down):
    token_single = tokens.astype(jnp.float32)
    gain_single = norm_gain.astype(jnp.float32)
    reciprocal_root_mean = lax.rsqrt(lax.optimization_barrier(jnp.mean(token_single * token_single, axis=1)) + 1e-05)
    standardized_input = token_single * reciprocal_root_mean[:, None]
    normalized_rows = (standardized_input * gain_single[None, :]).astype(jnp.bfloat16)
    pairs = TOKENS * TOP
    block_pairs = experts.reshape(N_SEQ, TOK_DEV * TOP)
    onehot = (block_pairs[:, :, None] == jnp.arange(EXPERTS, dtype=jnp.int32)[None, None, :]).astype(jnp.int32)
    rank = lax.optimization_barrier(jnp.sum((jnp.cumsum(onehot, axis=1) - 1) * onehot, axis=2))
    block_ids = jnp.arange(N_SEQ, dtype=jnp.int32)[:, None]
    position = (block_ids * CAP + rank).reshape(-1).astype(jnp.int32)
    pair_ids = jnp.arange(pairs, dtype=jnp.int32)
    table = jnp.full((EXPERTS, N_SEQ * CAP), pairs, jnp.int32)
    table = table.at[experts.reshape(-1), position].set(pair_ids)
    normed_pad = jnp.concatenate([normalized_rows, jnp.zeros((1, MODEL_WIDTH), jnp.bfloat16)], axis=0)
    upstream_pad = jnp.concatenate([upstream, jnp.zeros((1, MODEL_WIDTH), jnp.bfloat16)], axis=0)
    weights_pad = jnp.concatenate([route_weights.reshape(-1), jnp.zeros((1,), jnp.bfloat16)], axis=0)

    def per_expert(inputs):
        slot_assign, w_gu, w_dn = inputs
        token_rows = (slot_assign // TOP).astype(jnp.int32)
        grad_gu, grad_dn, grad_rows, weight_grad = expert_terms(normed_pad[token_rows], upstream_pad[token_rows], weights_pad[slot_assign], w_gu, w_dn)
        return (grad_gu.astype(jnp.bfloat16), grad_dn.astype(jnp.bfloat16), grad_rows, weight_grad)
    grad_gu, grad_dn, grad_rows, weight_grad = lax.map(per_expert, (table, w_gate_up, w_down))
    flat_table = table.reshape(-1)
    pair_grad = jnp.zeros((pairs + 1, MODEL_WIDTH), jnp.float32).at[flat_table].add(grad_rows.reshape(-1, MODEL_WIDTH))
    normed_gradient = lax.optimization_barrier(jnp.sum(pair_grad[:pairs].reshape(TOKENS, TOP, MODEL_WIDTH), axis=1))
    grad_weights = jnp.zeros((pairs + 1,), jnp.float32).at[flat_table].add(weight_grad.reshape(-1))[:pairs].reshape(TOKENS, TOP)
    correction_term = normed_gradient * gain_single[None, :]
    reduced_statistic = lax.optimization_barrier(jnp.sum(correction_term * standardized_input, axis=1)) / MODEL_WIDTH
    token_gradient = (upstream.astype(jnp.float32) + reciprocal_root_mean[:, None] * (correction_term - standardized_input * reduced_statistic[:, None])).astype(jnp.bfloat16)
    gain_gradient = lax.optimization_barrier(jnp.sum(normed_gradient * standardized_input, axis=0))
    grad_gate_up = grad_gu.reshape(EXPERTS, MODEL_WIDTH, 2, FF)
    return (token_gradient, gain_gradient, grad_weights, grad_gate_up, grad_dn)
```

```python
import jax
import jax.numpy as jnp
from jax import lax
from jax.experimental import pallas as pl
from jax.experimental.pallas import tpu as pltpu
from jax.sharding import PartitionSpec as P


def expert_terms(x_rows, dy_rows, weight_rows, w_gu, w_dn):
    width = x_rows.shape[1]
    hidden = w_dn.shape[0]
    flat_gu = w_gu.reshape(width, 2 * hidden)
    projected = jnp.dot(x_rows, flat_gu, preferred_element_type=jnp.float32)
    gate_pre = projected[:, :hidden]
    up_pre = projected[:, hidden:]
    sig_gate = jax.nn.sigmoid(1.702 * gate_pre)
    glu_value = gate_pre * sig_gate
    activated = ((up_pre + 1.0) * glu_value).astype(jnp.bfloat16)
    back_proj = lax.dot_general(
        dy_rows, w_dn, (((1,), (1,)), ((), ())), preferred_element_type=jnp.float32
    )
    row_weight = weight_rows.astype(jnp.float32)[:, None]
    weight_grad = jnp.sum(activated.astype(jnp.float32) * back_proj, axis=1)
    dact = row_weight * back_proj
    dgate_pre = dact * (up_pre + 1.0) * (sig_gate + 1.702 * gate_pre * sig_gate * (1.0 - sig_gate))
    dup_pre = dact * glu_value
    dproj = jnp.concatenate([dgate_pre, dup_pre], axis=1).astype(jnp.bfloat16)
    scaled = (row_weight * activated.astype(jnp.float32)).astype(jnp.bfloat16)
    grad_dn = lax.dot_general(
        scaled, dy_rows, (((0,), (0,)), ((), ())), preferred_element_type=jnp.float32
    )
    grad_gu = lax.dot_general(
        x_rows, dproj, (((0,), (0,)), ((), ())), preferred_element_type=jnp.float32
    )
    grad_rows = lax.dot_general(
        dproj, flat_gu, (((1,), (1,)), ((), ())), preferred_element_type=jnp.float32
    )
    return (grad_gu, grad_dn, grad_rows, weight_grad)


def earlier_same(pairs):
    count = pairs.shape[-1]
    same = pairs[..., :, None] == pairs[..., None, :]
    order = jnp.arange(count, dtype=jnp.int32)
    before = order[None, :] < order[:, None]
    return jnp.sum((same & before).astype(jnp.int32), axis=-1)


def plane_neighbours(me):
    core = me + 1 - 2 * (me % 2)
    across_x = me + 2 - 4 * ((me // 2) % 2)
    across_y = me + 4 - 8 * (me // 4)
    return core, across_x, across_y


def spread_kernel(depth, own_ref, out_ref, send_sem, recv_sem, copy_sem):
    z = lax.axis_index("dp")
    me = lax.axis_index("seq")
    core, ax, ay = plane_neighbours(me)
    diag = me + (ax - me) + (ay - me)

    barrier = pltpu.get_barrier_semaphore()
    for near in (core, ax, ay):
        pl.semaphore_signal(barrier, inc=1, device_id={"seq": near})
    for k in range(1, depth):
        pl.semaphore_signal(barrier, inc=1, device_id={"dp": (z + k) % depth})
    pl.semaphore_wait(barrier, 3 + depth - 1)

    kinds = 9
    started = {}

    def send(index, source, target, where):
        copy = pltpu.make_async_remote_copy(
            src_ref=source,
            dst_ref=target,
            send_sem=send_sem.at[index],
            recv_sem=recv_sem.at[index],
            device_id=where,
        )
        copy.start()
        started[index] = copy

    def origin(k):
        return (z + depth - k) % depth

    def arrived(k, kind):
        started[k * kinds + kind].wait_recv()

    def own(k):
        block = own_ref if k == 0 else out_ref.at[me, origin(k)]
        if k > 0:
            started[kinds * depth + k].wait_recv()
        target = out_ref.at[me, origin(k)]
        send(k * kinds + 0, block, target, {"seq": ax})
        send(k * kinds + 1, block, target, {"seq": ay})
        send(k * kinds + 2, block, target, {"seq": core})

    def relay(k):
        zs = origin(k)
        arrived(k, 0)
        from_x = out_ref.at[ax, zs]
        send(k * kinds + 3, from_x.at[0], from_x.at[0], {"seq": ay})
        arrived(k, 1)
        from_y = out_ref.at[ay, zs]
        send(k * kinds + 4, from_y.at[1], from_y.at[1], {"seq": ax})
        send(k * kinds + 5, from_x, from_x, {"seq": core})
        send(k * kinds + 6, from_y, from_y, {"seq": core})

    def corner(k):
        zs = origin(k)
        far = out_ref.at[diag, zs]
        arrived(k, 3)
        send(k * kinds + 7, far.at[0], far.at[0], {"seq": core})
        arrived(k, 4)
        send(k * kinds + 8, far.at[1], far.at[1], {"seq": core})

    for k in range(1, depth):
        send(kinds * depth + k, own_ref, out_ref.at[me, z], {"dp": (z + k) % depth})
    keep = pltpu.make_async_copy(own_ref, out_ref.at[me, z], copy_sem)
    keep.start()
    for step in range(depth + 2):
        if step < depth:
            own(step)
        if 1 <= step <= depth:
            relay(step - 1)
        if 2 <= step:
            corner(step - 2)
    for k in range(depth):
        for kind in (2, 5, 6, 7, 8):
            arrived(k, kind)
    for copy in started.values():
        copy.wait_send()
    keep.wait()


def spread(block, depth, peers):
    count = 9 * depth + depth
    return pl.pallas_call(
        lambda *refs: spread_kernel(depth, *refs),
        out_shape=jax.ShapeDtypeStruct((peers, depth) + block.shape, block.dtype),
        in_specs=[pl.BlockSpec(memory_space=pl.ANY)],
        out_specs=pl.BlockSpec(memory_space=pl.ANY),
        scratch_shapes=[
            pltpu.SemaphoreType.DMA((count,)),
            pltpu.SemaphoreType.DMA((count,)),
            pltpu.SemaphoreType.DMA,
        ],
        compiler_params=pltpu.CompilerParams(collective_id=0, has_side_effects=True),
        name="spread",
    )(block)


def fill_kernel(depth, part, got_ref, select_ref, gain_ref, x_ref, dy_ref):
    members, _, capacity, _ = x_ref.shape
    select = select_ref[0]
    total = None
    for z in range(depth):
        piece = got_ref[0, z, 0, :, :part].astype(jnp.float32)
        square = jnp.sum(piece * piece, axis=1, keepdims=True)
        total = square if total is None else total + square
    inv = lax.rsqrt(total / (part * depth) + 1e-05)
    for z in range(depth):
        at = slice(z * part, (z + 1) * part)
        piece = got_ref[0, z, 0, :, :part].astype(jnp.float32)
        normed = (piece * inv * gain_ref[:, at]).astype(jnp.bfloat16)
        for source, target in ((normed, x_ref), (got_ref[0, z, 1, :, :part], dy_ref)):
            chosen = jnp.dot(select, source, preferred_element_type=jnp.float32).astype(
                jnp.bfloat16
            )
            for m in range(members):
                target[m, 0, :, at] = chosen[m * capacity : (m + 1) * capacity]


def fill_slots(got, select, gain, part, members, capacity):
    peers, depth, _, rows, lanes = got.shape
    width = part * depth
    made = jax.ShapeDtypeStruct((members, peers, capacity, width), jnp.bfloat16)
    out = pl.BlockSpec((members, 1, capacity, width), lambda b: (0, b, 0, 0))
    return pl.pallas_call(
        lambda *refs: fill_kernel(depth, part, *refs),
        grid=(peers,),
        out_shape=(made, made),
        in_specs=[
            pl.BlockSpec((1, depth, 2, rows, lanes), lambda b: (b, 0, 0, 0, 0)),
            pl.BlockSpec((1,) + select.shape[1:], lambda b: (b, 0, 0)),
            pl.BlockSpec((1, width), lambda b: (0, 0)),
        ],
        out_specs=(out, out),
        compiler_params=pltpu.CompilerParams(vmem_limit_bytes=32 * 2**20),
        name="fill_slots",
    )(got, select, gain[None, :])


def exchange_kernel(depth, peers, stat_ref, gain_ref, stats_ref, gains_ref, sends, lands, keeps):
    z = lax.axis_index("dp")
    me = lax.axis_index("seq")
    barrier = pltpu.get_barrier_semaphore()
    for k in range(1, depth):
        pl.semaphore_signal(barrier, inc=1, device_id={"dp": (z + k) % depth})
    for k in range(1, peers):
        pl.semaphore_signal(barrier, inc=1, device_id={"seq": (me + k) % peers})
    pl.semaphore_wait(barrier, depth + peers - 2)
    copies = []
    for k in range(1, depth):
        where = {"dp": (z + k) % depth}
        copies.append((stat_ref, stats_ref.at[k], where))
    for k in range(1, peers):
        where = {"seq": (me + k) % peers}
        copies.append((gain_ref, gains_ref.at[k], where))
    running = []
    for n, (source, target, where) in enumerate(copies):
        copy = pltpu.make_async_remote_copy(
            src_ref=source,
            dst_ref=target,
            send_sem=sends.at[n],
            recv_sem=lands.at[n],
            device_id=where,
        )
        copy.start()
        running.append(copy)
    for n, (source, target) in enumerate(((stat_ref, stats_ref), (gain_ref, gains_ref))):
        copy = pltpu.make_async_copy(source, target.at[0], keeps.at[n])
        copy.start()
        running.append(copy)
    for copy in running:
        copy.wait()


def exchange(stat, gain, depth, peers):
    count = depth + peers - 2
    return pl.pallas_call(
        lambda *refs: exchange_kernel(depth, peers, *refs),
        out_shape=(
            jax.ShapeDtypeStruct((depth,) + stat.shape, stat.dtype),
            jax.ShapeDtypeStruct((peers,) + gain.shape, gain.dtype),
        ),
        in_specs=[pl.BlockSpec(memory_space=pltpu.VMEM)] * 2,
        out_specs=(pl.BlockSpec(memory_space=pltpu.VMEM),) * 2,
        scratch_shapes=[
            pltpu.SemaphoreType.DMA((count,)),
            pltpu.SemaphoreType.DMA((count,)),
            pltpu.SemaphoreType.DMA((2,)),
        ],
        compiler_params=pltpu.CompilerParams(collective_id=1, has_side_effects=True),
        name="exchange",
    )(stat, gain)


def plane_body(tokens, upstream, norm_gain, experts, route_weights, w_gate_up, w_down):
    dp_count = lax.axis_size("dp")
    seq_count = lax.axis_size("seq")
    rows, part = tokens.shape
    width = part * dp_count
    top = experts.shape[1]
    exp_local = w_gate_up.shape[0]
    hidden = w_down.shape[1]
    exp_total = exp_local * seq_count
    capacity = rows * top * 3 // (2 * exp_total)
    slots = exp_local * capacity
    everyone = seq_count * rows
    me = lax.axis_index("seq")
    lanes = -(-(part + 2 * top) // 128) * 128
    room = lanes - part - 2 * top
    fill = jnp.zeros((rows, room), jnp.bfloat16)
    mine = jnp.stack(
        [
            jnp.concatenate([tokens, experts.astype(jnp.bfloat16), route_weights, fill], axis=1),
            jnp.concatenate(
                [upstream, jnp.zeros((rows, 2 * top), jnp.bfloat16), fill], axis=1
            ),
        ]
    )
    got = spread(mine, dp_count, seq_count)
    all_experts = got[:, 0, 0, :, part : part + top].astype(jnp.int32).reshape(seq_count, -1)
    all_weights = got[:, 0, 0, :, part + top : part + 2 * top].reshape(seq_count, -1)
    rank = earlier_same(all_experts)

    gain = norm_gain.astype(jnp.float32)
    own_tok = lax.dynamic_index_in_dim(got, me, 0, keepdims=False)[:, 0, :, :part].astype(
        jnp.float32
    )
    my_inv = lax.rsqrt(jnp.sum(own_tok * own_tok, axis=(0, 2)) / width + 1e-05)[:, None]

    local = all_experts - me * exp_local
    place = jnp.where((local >= 0) & (local < exp_local), local * capacity + rank, -1)
    place = place.reshape(seq_count, rows, top)
    numbers = jnp.arange(slots, dtype=jnp.int32)
    hits = jnp.swapaxes(place, 1, 2)[:, :, None, :] == numbers[None, None, :, None]
    select = jnp.sum(hits.astype(jnp.float32), axis=1).astype(jnp.bfloat16)
    weights = jnp.swapaxes(
        all_weights.reshape(seq_count, rows, top).astype(jnp.float32), 1, 2
    )
    slot_weight = jnp.sum(jnp.where(hits, weights[:, :, None, :], 0.0), axis=(1, 3))
    slot_weight = jnp.swapaxes(
        slot_weight.astype(jnp.bfloat16).reshape(seq_count, exp_local, capacity), 0, 1
    ).reshape(-1)
    x_all, dy_all = fill_slots(got, select, gain, part, exp_local, capacity)
    x_all = x_all.reshape(-1, width)
    dy_all = dy_all.reshape(-1, width)
    member_rows = seq_count * capacity
    grads_gu, grads_dn, back_rows, back_weights = [], [], [], []
    for member in range(exp_local):
        at = slice(member * member_rows, (member + 1) * member_rows)
        g_gu, g_dn, g_rows, g_weight = expert_terms(
            x_all[at], dy_all[at], slot_weight[at], w_gate_up[member], w_down[member]
        )
        grads_gu.append(g_gu.reshape(width, 2, hidden).astype(jnp.bfloat16))
        grads_dn.append(g_dn.astype(jnp.bfloat16))
        back_rows.append(g_rows.astype(jnp.bfloat16).reshape(seq_count, capacity, width))
        back_weights.append(g_weight.reshape(seq_count, capacity, 1))
    high = [w.astype(jnp.bfloat16) for w in back_weights]
    low = [(w - h.astype(jnp.float32)).astype(jnp.bfloat16) for w, h in zip(back_weights, high)]
    leaving = jnp.concatenate(
        [jnp.concatenate(t, axis=2) for t in zip(back_rows, high, low)], axis=1
    )
    home = lax.all_to_all(leaving, "seq", split_axis=0, concat_axis=0, tiled=True)
    home = home.reshape(seq_count * slots, width + 2)
    my_experts = experts.reshape(-1)
    spot = (my_experts * capacity + earlier_same(my_experts)).reshape(rows, top)
    mover = jnp.sum(
        (spot[:, :, None] == jnp.arange(seq_count * slots, dtype=jnp.int32)).astype(jnp.float32),
        axis=1,
    ).astype(jnp.bfloat16)
    combined = jnp.dot(mover, home[:, :width], preferred_element_type=jnp.float32)
    came = home[:, width].astype(jnp.float32) + home[:, width + 1].astype(jnp.float32)
    pair_weight = jnp.sum(
        jnp.where(
            spot[:, :, None] == jnp.arange(seq_count * slots, dtype=jnp.int32),
            came[None, None, :],
            0.0,
        ),
        axis=2,
    )
    dnormed = lax.psum_scatter(
        combined.astype(jnp.bfloat16), "dp", scatter_dimension=1, tiled=True
    ).astype(jnp.float32)
    my_gain = lax.dynamic_slice_in_dim(gain, lax.axis_index("dp") * part, part, 0)
    xhat = tokens.astype(jnp.float32) * my_inv
    u = dnormed * my_gain[None, :]
    small = jnp.concatenate([jnp.sum(u * xhat, axis=1)[:, None], pair_weight], axis=1)
    tile = 8 * 128
    stat_tiles = -(-small.size // tile)
    stat_block = jnp.pad(small.T.reshape(-1), (0, stat_tiles * tile - small.size))
    gain_part = jnp.sum(dnormed * xhat, axis=0)
    gain_tiles = -(-part // tile)
    gain_block = jnp.pad(gain_part, (0, gain_tiles * tile - part))
    stat_all, gain_all = exchange(
        stat_block.reshape(stat_tiles * 8, 128),
        gain_block.reshape(gain_tiles * 8, 128),
        dp_count,
        seq_count,
    )
    both = jnp.sum(stat_all, axis=0).reshape(-1)[: small.size].reshape(1 + top, rows).T
    gain_gradient = jnp.sum(gain_all, axis=0).reshape(-1)[:part]
    stat = both[:, :1] / width
    token_gradient = (upstream.astype(jnp.float32) + my_inv * (u - xhat * stat)).astype(
        jnp.bfloat16
    )
    return (
        token_gradient,
        gain_gradient,
        both[:, 1:],
        jnp.stack(grads_gu, axis=0),
        jnp.stack(grads_dn, axis=0),
    )

def body(tokens, upstream, norm_gain, experts, route_weights, w_gate_up, w_down):
    dp_count = lax.axis_size("dp")
    seq_count = lax.axis_size("seq")
    token_row_list, part_width = tokens.shape
    width = part_width * dp_count
    picked_count = experts.shape[1]
    exp_local = w_gate_up.shape[0]
    hidden = w_down.shape[1]
    exp_total = exp_local * seq_count
    capacity = token_row_list * picked_count * 3 // (2 * exp_total)
    slot_total = exp_total * capacity
    gain_single = norm_gain.astype(jnp.float32)
    gain_part = lax.dynamic_slice_in_dim(
        gain_single, lax.axis_index("dp") * part_width, part_width, 0
    )
    token_piece = tokens.astype(jnp.float32)
    pair_experts = experts.reshape(-1)
    rank = earlier_same(pair_experts)
    position = pair_experts * capacity + rank
    placing = (position[None, :] == jnp.arange(slot_total, dtype=jnp.int32)[:, None]).astype(
        jnp.bfloat16
    )
    mover = jnp.sum(placing.reshape(slot_total, token_row_list, picked_count), axis=2)
    slot_weights = jnp.dot(
        placing, route_weights.reshape(-1), preferred_element_type=jnp.float32
    ).astype(jnp.bfloat16)
    full_tok, full_dy = (
        lax.all_gather(tokens, "dp", axis=1, tiled=True),
        lax.all_gather(upstream, "dp", axis=1, tiled=True),
    )
    full_f32 = full_tok.astype(jnp.float32)
    reciprocal_root_mean = lax.rsqrt(jnp.mean(full_f32 * full_f32, axis=1) + 1e-05)
    normalized_rows = (full_f32 * reciprocal_root_mean[:, None] * gain_single[None, :]).astype(
        jnp.bfloat16
    )
    send_tok = jnp.dot(mover, normalized_rows, preferred_element_type=jnp.float32).astype(
        jnp.bfloat16
    )
    send_dy = jnp.dot(mover, full_dy, preferred_element_type=jnp.float32).astype(jnp.bfloat16)
    feat_width = send_tok.shape[1]
    got_tok, got_dy, got_weight = (
        lax.all_to_all(
            send_tok.reshape(exp_total, capacity, feat_width),
            "seq",
            split_axis=0,
            concat_axis=0,
            tiled=True,
        ),
        lax.all_to_all(
            send_dy.reshape(exp_total, capacity, feat_width),
            "seq",
            split_axis=0,
            concat_axis=0,
            tiled=True,
        ),
        lax.all_to_all(
            slot_weights.reshape(exp_total, capacity),
            "seq",
            split_axis=0,
            concat_axis=0,
            tiled=True,
        ),
    )
    got_tok = got_tok.reshape(seq_count, exp_local, capacity, feat_width)
    got_dy = got_dy.reshape(seq_count, exp_local, capacity, feat_width)
    got_weight = got_weight.reshape(seq_count, exp_local, capacity)
    grads_gu = []
    grads_dn = []
    rows_list = []
    weight_list = []
    for member in range(exp_local):
        x_rows = got_tok[:, member].reshape(seq_count * capacity, width)
        dy_rows = got_dy[:, member].reshape(seq_count * capacity, width)
        weight_rows = got_weight[:, member].reshape(seq_count * capacity)
        results = expert_terms(x_rows, dy_rows, weight_rows, w_gate_up[member], w_down[member])
        grads_gu.append(results[0].reshape(width, 2, hidden).astype(jnp.bfloat16))
        grads_dn.append(results[1].astype(jnp.bfloat16))
        rows_list.append(results[2].reshape(seq_count, capacity, width))
        weight_list.append(results[3].reshape(seq_count, capacity))
    rows_stack = jnp.stack(rows_list, axis=1).reshape(exp_total, capacity, width)
    weight_stack = jnp.stack(weight_list, axis=1).reshape(exp_total, capacity)
    back_rows, back_weight = (
        lax.all_to_all(
            rows_stack.astype(jnp.bfloat16), "seq", split_axis=0, concat_axis=0, tiled=True
        ).astype(rows_stack.dtype),
        lax.all_to_all(
            weight_stack.astype(jnp.bfloat16), "seq", split_axis=0, concat_axis=0, tiled=True
        ).astype(weight_stack.dtype),
    )
    combined = lax.dot_general(
        mover.astype(jnp.float32),
        back_rows.reshape(slot_total, back_rows.shape[2]),
        (((0,), (0,)), ((), ())),
        precision=lax.Precision.HIGHEST,
        preferred_element_type=jnp.float32,
    )
    pairing_weight = lax.dot_general(
        placing.astype(jnp.float32),
        back_weight.reshape(slot_total),
        (((0,), (0,)), ((), ())),
        precision=lax.Precision.HIGHEST,
        preferred_element_type=jnp.float32,
    )
    normed_gradient_piece = lax.psum_scatter(
        combined.astype(jnp.bfloat16), "dp", scatter_dimension=1, tiled=True
    ).astype(jnp.float32)
    standardized_piece = token_piece * reciprocal_root_mean[:, None]
    correction_term = normed_gradient_piece * gain_part[None, :]
    stat_sum, grad_weights = lax.psum(
        (
            jnp.sum(correction_term * standardized_piece, axis=1),
            pairing_weight.reshape(token_row_list, picked_count),
        ),
        "dp",
    )
    reduced_statistic = stat_sum / width
    token_gradient = (
        upstream.astype(jnp.float32)
        + reciprocal_root_mean[:, None]
        * (correction_term - standardized_piece * reduced_statistic[:, None])
    ).astype(jnp.bfloat16)
    gain_gradient = lax.psum(jnp.sum(normed_gradient_piece * standardized_piece, axis=0), "seq")
    grad_gate_up = jnp.stack(grads_gu, axis=0)
    grad_down = jnp.stack(grads_dn, axis=0)
    return (token_gradient, gain_gradient, grad_weights, grad_gate_up, grad_down)


def solution(mesh):
    in_specs = (
        P("seq", "dp"),
        P("seq", "dp"),
        P(),
        P("seq", None),
        P("seq", None),
        P("seq", None, None, "dp"),
        P("seq", "dp", None),
    )
    out_specs = (
        P("seq", "dp"),
        P("dp"),
        P("seq", None),
        P("seq", None, None, "dp"),
        P("seq", "dp", None),
    )
    fast = mesh.shape["seq"] == 8 and mesh.shape["dp"] > 1
    return jax.shard_map(plane_body if fast else body, mesh=mesh, in_specs=in_specs, out_specs=out_specs, check_vma=False)
```

```python
import jax
import jax.numpy as jnp
from jax import lax
from jax.experimental import pallas as pl
from jax.experimental.pallas import tpu as pltpu
from jax.sharding import PartitionSpec as P


def expert_terms(x_rows, dy_rows, weight_rows, w_gu, w_dn):
    width = x_rows.shape[1]
    hidden = w_dn.shape[0]
    flat_gu = w_gu.reshape(width, 2 * hidden)
    projected = jnp.dot(x_rows, flat_gu, preferred_element_type=jnp.float32)
    gate_pre = projected[:, :hidden]
    up_pre = projected[:, hidden:]
    sig_gate = jax.nn.sigmoid(1.702 * gate_pre)
    glu_value = gate_pre * sig_gate
    activated = ((up_pre + 1.0) * glu_value).astype(jnp.bfloat16)
    back_proj = lax.dot_general(
        dy_rows, w_dn, (((1,), (1,)), ((), ())), preferred_element_type=jnp.float32
    )
    row_weight = weight_rows.astype(jnp.float32)[:, None]
    weight_grad = jnp.sum(activated.astype(jnp.float32) * back_proj, axis=1)
    dact = row_weight * back_proj
    dgate_pre = dact * (up_pre + 1.0) * (sig_gate + 1.702 * gate_pre * sig_gate * (1.0 - sig_gate))
    dup_pre = dact * glu_value
    dproj = jnp.concatenate([dgate_pre, dup_pre], axis=1).astype(jnp.bfloat16)
    scaled = (row_weight * activated.astype(jnp.float32)).astype(jnp.bfloat16)
    grad_dn = lax.dot_general(
        scaled, dy_rows, (((0,), (0,)), ((), ())), preferred_element_type=jnp.float32
    )
    grad_gu = lax.dot_general(
        x_rows, dproj, (((0,), (0,)), ((), ())), preferred_element_type=jnp.float32
    )
    grad_rows = lax.dot_general(
        dproj, flat_gu, (((1,), (1,)), ((), ())), preferred_element_type=jnp.float32
    )
    return (grad_gu, grad_dn, grad_rows, weight_grad)


def earlier_same(pairs):
    count = pairs.shape[-1]
    same = pairs[..., :, None] == pairs[..., None, :]
    order = jnp.arange(count, dtype=jnp.int32)
    before = order[None, :] < order[:, None]
    return jnp.sum((same & before).astype(jnp.int32), axis=-1)


def plane_neighbours(me):
    core = me + 1 - 2 * (me % 2)
    across_x = me + 2 - 4 * ((me // 2) % 2)
    across_y = me + 4 - 8 * (me // 4)
    return core, across_x, across_y


def spread_kernel(depth, own_ref, out_ref, send_sem, recv_sem, copy_sem):
    z = lax.axis_index("dp")
    me = lax.axis_index("seq")
    core, ax, ay = plane_neighbours(me)
    diag = me + (ax - me) + (ay - me)

    barrier = pltpu.get_barrier_semaphore()
    for near in (core, ax, ay):
        pl.semaphore_signal(barrier, inc=1, device_id={"seq": near})
    for k in range(1, depth):
        pl.semaphore_signal(barrier, inc=1, device_id={"dp": (z + k) % depth})
    pl.semaphore_wait(barrier, 3 + depth - 1)

    kinds = 9
    started = {}

    def send(index, source, target, where):
        copy = pltpu.make_async_remote_copy(
            src_ref=source,
            dst_ref=target,
            send_sem=send_sem.at[index],
            recv_sem=recv_sem.at[index],
            device_id=where,
        )
        copy.start()
        started[index] = copy

    def origin(k):
        return (z + depth - k) % depth

    def arrived(k, kind):
        started[k * kinds + kind].wait_recv()

    def own(k):
        block = own_ref if k == 0 else out_ref.at[me, origin(k)]
        if k > 0:
            started[kinds * depth + k].wait_recv()
        target = out_ref.at[me, origin(k)]
        send(k * kinds + 0, block, target, {"seq": ax})
        send(k * kinds + 1, block, target, {"seq": ay})
        send(k * kinds + 2, block, target, {"seq": core})

    def relay(k):
        zs = origin(k)
        arrived(k, 0)
        from_x = out_ref.at[ax, zs]
        send(k * kinds + 3, from_x.at[0], from_x.at[0], {"seq": ay})
        arrived(k, 1)
        from_y = out_ref.at[ay, zs]
        send(k * kinds + 4, from_y.at[1], from_y.at[1], {"seq": ax})
        send(k * kinds + 5, from_x, from_x, {"seq": core})
        send(k * kinds + 6, from_y, from_y, {"seq": core})

    def corner(k):
        zs = origin(k)
        far = out_ref.at[diag, zs]
        arrived(k, 3)
        send(k * kinds + 7, far.at[0], far.at[0], {"seq": core})
        arrived(k, 4)
        send(k * kinds + 8, far.at[1], far.at[1], {"seq": core})

    for k in range(1, depth):
        send(kinds * depth + k, own_ref, out_ref.at[me, z], {"dp": (z + k) % depth})
    keep = pltpu.make_async_copy(own_ref, out_ref.at[me, z], copy_sem)
    keep.start()
    for step in range(depth + 2):
        if step < depth:
            own(step)
        if 1 <= step <= depth:
            relay(step - 1)
        if 2 <= step:
            corner(step - 2)
    for k in range(depth):
        for kind in (2, 5, 6, 7, 8):
            arrived(k, kind)
    for copy in started.values():
        copy.wait_send()
    keep.wait()


def spread(block, depth, peers):
    count = 9 * depth + depth
    return pl.pallas_call(
        lambda *refs: spread_kernel(depth, *refs),
        out_shape=jax.ShapeDtypeStruct((peers, depth) + block.shape, block.dtype),
        in_specs=[pl.BlockSpec(memory_space=pl.ANY)],
        out_specs=pl.BlockSpec(memory_space=pl.ANY),
        scratch_shapes=[
            pltpu.SemaphoreType.DMA((count,)),
            pltpu.SemaphoreType.DMA((count,)),
            pltpu.SemaphoreType.DMA,
        ],
        compiler_params=pltpu.CompilerParams(collective_id=0, has_side_effects=True),
        name="spread",
    )(block)


def fill_kernel(depth, part, got_ref, select_ref, gain_ref, x_ref, dy_ref):
    members, _, capacity, _ = x_ref.shape
    select = select_ref[0]
    total = None
    for z in range(depth):
        piece = got_ref[0, z, 0, :, :part].astype(jnp.float32)
        square = jnp.sum(piece * piece, axis=1, keepdims=True)
        total = square if total is None else total + square
    inv = lax.rsqrt(total / (part * depth) + 1e-05)
    for z in range(depth):
        at = slice(z * part, (z + 1) * part)
        piece = got_ref[0, z, 0, :, :part].astype(jnp.float32)
        normed = (piece * inv * gain_ref[:, at]).astype(jnp.bfloat16)
        for source, target in ((normed, x_ref), (got_ref[0, z, 1, :, :part], dy_ref)):
            chosen = jnp.dot(select, source, preferred_element_type=jnp.float32).astype(
                jnp.bfloat16
            )
            for m in range(members):
                target[m, 0, :, at] = chosen[m * capacity : (m + 1) * capacity]


def fill_slots(got, select, gain, part, members, capacity):
    peers, depth, _, rows, lanes = got.shape
    width = part * depth
    made = jax.ShapeDtypeStruct((members, peers, capacity, width), jnp.bfloat16)
    out = pl.BlockSpec((members, 1, capacity, width), lambda b: (0, b, 0, 0))
    return pl.pallas_call(
        lambda *refs: fill_kernel(depth, part, *refs),
        grid=(peers,),
        out_shape=(made, made),
        in_specs=[
            pl.BlockSpec((1, depth, 2, rows, lanes), lambda b: (b, 0, 0, 0, 0)),
            pl.BlockSpec((1,) + select.shape[1:], lambda b: (b, 0, 0)),
            pl.BlockSpec((1, width), lambda b: (0, 0)),
        ],
        out_specs=(out, out),
        compiler_params=pltpu.CompilerParams(vmem_limit_bytes=32 * 2**20),
        name="fill_slots",
    )(got, select, gain[None, :])


def exchange_kernel(depth, peers, stat_ref, gain_ref, stats_ref, gains_ref, sends, lands, keeps):
    z = lax.axis_index("dp")
    me = lax.axis_index("seq")
    barrier = pltpu.get_barrier_semaphore()
    for k in range(1, depth):
        pl.semaphore_signal(barrier, inc=1, device_id={"dp": (z + k) % depth})
    for k in range(1, peers):
        pl.semaphore_signal(barrier, inc=1, device_id={"seq": (me + k) % peers})
    pl.semaphore_wait(barrier, depth + peers - 2)
    copies = []
    for k in range(1, depth):
        where = {"dp": (z + k) % depth}
        copies.append((stat_ref, stats_ref.at[k], where))
    for k in range(1, peers):
        where = {"seq": (me + k) % peers}
        copies.append((gain_ref, gains_ref.at[k], where))
    running = []
    for n, (source, target, where) in enumerate(copies):
        copy = pltpu.make_async_remote_copy(
            src_ref=source,
            dst_ref=target,
            send_sem=sends.at[n],
            recv_sem=lands.at[n],
            device_id=where,
        )
        copy.start()
        running.append(copy)
    for n, (source, target) in enumerate(((stat_ref, stats_ref), (gain_ref, gains_ref))):
        copy = pltpu.make_async_copy(source, target.at[0], keeps.at[n])
        copy.start()
        running.append(copy)
    for copy in running:
        copy.wait()


def exchange(stat, gain, depth, peers):
    count = depth + peers - 2
    return pl.pallas_call(
        lambda *refs: exchange_kernel(depth, peers, *refs),
        out_shape=(
            jax.ShapeDtypeStruct((depth,) + stat.shape, stat.dtype),
            jax.ShapeDtypeStruct((peers,) + gain.shape, gain.dtype),
        ),
        in_specs=[pl.BlockSpec(memory_space=pltpu.VMEM)] * 2,
        out_specs=(pl.BlockSpec(memory_space=pltpu.VMEM),) * 2,
        scratch_shapes=[
            pltpu.SemaphoreType.DMA((count,)),
            pltpu.SemaphoreType.DMA((count,)),
            pltpu.SemaphoreType.DMA((2,)),
        ],
        compiler_params=pltpu.CompilerParams(collective_id=1, has_side_effects=True),
        name="exchange",
    )(stat, gain)


def scatter_kernel(depth, pieces_ref, out_ref, sends, lands, keep):
    z = lax.axis_index("dp")
    barrier = pltpu.get_barrier_semaphore()
    for k in range(1, depth):
        pl.semaphore_signal(barrier, inc=1, device_id={"dp": (z + k) % depth})
    pl.semaphore_wait(barrier, depth - 1)
    running = []
    for k in range(1, depth):
        copy = pltpu.make_async_remote_copy(
            src_ref=pieces_ref.at[(z + k) % depth],
            dst_ref=out_ref.at[k],
            send_sem=sends.at[k],
            recv_sem=lands.at[k],
            device_id={"dp": (z + k) % depth},
        )
        copy.start()
        running.append(copy)
    copy = pltpu.make_async_copy(pieces_ref.at[z], out_ref.at[0], keep)
    copy.start()
    running.append(copy)
    for copy in running:
        copy.wait()


def scatter(pieces):
    depth = pieces.shape[0]
    return pl.pallas_call(
        lambda *refs: scatter_kernel(depth, *refs),
        out_shape=jax.ShapeDtypeStruct(pieces.shape, pieces.dtype),
        in_specs=[pl.BlockSpec(memory_space=pltpu.VMEM)],
        out_specs=pl.BlockSpec(memory_space=pltpu.VMEM),
        scratch_shapes=[
            pltpu.SemaphoreType.DMA((depth,)),
            pltpu.SemaphoreType.DMA((depth,)),
            pltpu.SemaphoreType.DMA,
        ],
        compiler_params=pltpu.CompilerParams(collective_id=2, has_side_effects=True),
        name="scatter",
    )(pieces)


def plane_body(tokens, upstream, norm_gain, experts, route_weights, w_gate_up, w_down):
    dp_count = lax.axis_size("dp")
    seq_count = lax.axis_size("seq")
    rows, part = tokens.shape
    width = part * dp_count
    top = experts.shape[1]
    exp_local = w_gate_up.shape[0]
    hidden = w_down.shape[1]
    exp_total = exp_local * seq_count
    capacity = rows * top * 3 // (2 * exp_total)
    slots = exp_local * capacity
    everyone = seq_count * rows
    me = lax.axis_index("seq")
    lanes = -(-(part + 2 * top) // 128) * 128
    room = lanes - part - 2 * top
    fill = jnp.zeros((rows, room), jnp.bfloat16)
    mine = jnp.stack(
        [
            jnp.concatenate([tokens, experts.astype(jnp.bfloat16), route_weights, fill], axis=1),
            jnp.concatenate(
                [upstream, jnp.zeros((rows, 2 * top), jnp.bfloat16), fill], axis=1
            ),
        ]
    )
    got = spread(mine, dp_count, seq_count)
    all_experts = got[:, 0, 0, :, part : part + top].astype(jnp.int32).reshape(seq_count, -1)
    all_weights = got[:, 0, 0, :, part + top : part + 2 * top].reshape(seq_count, -1)
    rank = earlier_same(all_experts)

    gain = norm_gain.astype(jnp.float32)
    own_tok = lax.dynamic_index_in_dim(got, me, 0, keepdims=False)[:, 0, :, :part].astype(
        jnp.float32
    )
    my_inv = lax.rsqrt(jnp.sum(own_tok * own_tok, axis=(0, 2)) / width + 1e-05)[:, None]

    local = all_experts - me * exp_local
    place = jnp.where((local >= 0) & (local < exp_local), local * capacity + rank, -1)
    place = place.reshape(seq_count, rows, top)
    numbers = jnp.arange(slots, dtype=jnp.int32)
    hits = jnp.swapaxes(place, 1, 2)[:, :, None, :] == numbers[None, None, :, None]
    select = jnp.sum(hits.astype(jnp.float32), axis=1).astype(jnp.bfloat16)
    weights = jnp.swapaxes(
        all_weights.reshape(seq_count, rows, top).astype(jnp.float32), 1, 2
    )
    slot_weight = jnp.sum(jnp.where(hits, weights[:, :, None, :], 0.0), axis=(1, 3))
    slot_weight = jnp.swapaxes(
        slot_weight.astype(jnp.bfloat16).reshape(seq_count, exp_local, capacity), 0, 1
    ).reshape(-1)
    x_all, dy_all = fill_slots(got, select, gain, part, exp_local, capacity)
    x_all = x_all.reshape(-1, width)
    dy_all = dy_all.reshape(-1, width)
    member_rows = seq_count * capacity
    grads_gu, grads_dn, back_rows, back_weights = [], [], [], []
    for member in range(exp_local):
        at = slice(member * member_rows, (member + 1) * member_rows)
        g_gu, g_dn, g_rows, g_weight = expert_terms(
            x_all[at], dy_all[at], slot_weight[at], w_gate_up[member], w_down[member]
        )
        grads_gu.append(g_gu.reshape(width, 2, hidden).astype(jnp.bfloat16))
        grads_dn.append(g_dn.astype(jnp.bfloat16))
        back_rows.append(g_rows.astype(jnp.bfloat16).reshape(seq_count, capacity, width))
        back_weights.append(g_weight.reshape(seq_count, capacity, 1))
    high = [w.astype(jnp.bfloat16) for w in back_weights]
    low = [(w - h.astype(jnp.float32)).astype(jnp.bfloat16) for w, h in zip(back_weights, high)]
    leaving = jnp.concatenate(
        [jnp.concatenate(t, axis=2) for t in zip(back_rows, high, low)], axis=1
    )
    home = lax.all_to_all(leaving, "seq", split_axis=0, concat_axis=0, tiled=True)
    home = home.reshape(seq_count * slots, width + 2)
    my_experts = experts.reshape(-1)
    spot = (my_experts * capacity + earlier_same(my_experts)).reshape(rows, top)
    mover = jnp.sum(
        (spot[:, :, None] == jnp.arange(seq_count * slots, dtype=jnp.int32)).astype(jnp.float32),
        axis=1,
    ).astype(jnp.bfloat16)
    combined = jnp.dot(mover, home[:, :width], preferred_element_type=jnp.float32)
    came = home[:, width].astype(jnp.float32) + home[:, width + 1].astype(jnp.float32)
    pair_weight = jnp.sum(
        jnp.where(
            spot[:, :, None] == jnp.arange(seq_count * slots, dtype=jnp.int32),
            came[None, None, :],
            0.0,
        ),
        axis=2,
    )
    pieces = jnp.stack(jnp.split(combined.astype(jnp.bfloat16), dp_count, axis=1))
    dnormed = jnp.sum(scatter(pieces).astype(jnp.float32), axis=0)
    my_gain = lax.dynamic_slice_in_dim(gain, lax.axis_index("dp") * part, part, 0)
    xhat = tokens.astype(jnp.float32) * my_inv
    u = dnormed * my_gain[None, :]
    small = jnp.concatenate([jnp.sum(u * xhat, axis=1)[:, None], pair_weight], axis=1)
    tile = 8 * 128
    stat_tiles = -(-small.size // tile)
    stat_block = jnp.pad(small.T.reshape(-1), (0, stat_tiles * tile - small.size))
    gain_part = jnp.sum(dnormed * xhat, axis=0)
    gain_tiles = -(-part // tile)
    gain_block = jnp.pad(gain_part, (0, gain_tiles * tile - part))
    stat_all, gain_all = exchange(
        stat_block.reshape(stat_tiles * 8, 128),
        gain_block.reshape(gain_tiles * 8, 128),
        dp_count,
        seq_count,
    )
    both = jnp.sum(stat_all, axis=0).reshape(-1)[: small.size].reshape(1 + top, rows).T
    gain_gradient = jnp.sum(gain_all, axis=0).reshape(-1)[:part]
    stat = both[:, :1] / width
    token_gradient = (upstream.astype(jnp.float32) + my_inv * (u - xhat * stat)).astype(
        jnp.bfloat16
    )
    return (
        token_gradient,
        gain_gradient,
        both[:, 1:],
        jnp.stack(grads_gu, axis=0),
        jnp.stack(grads_dn, axis=0),
    )

def body(tokens, upstream, norm_gain, experts, route_weights, w_gate_up, w_down):
    dp_count = lax.axis_size("dp")
    seq_count = lax.axis_size("seq")
    token_row_list, part_width = tokens.shape
    width = part_width * dp_count
    picked_count = experts.shape[1]
    exp_local = w_gate_up.shape[0]
    hidden = w_down.shape[1]
    exp_total = exp_local * seq_count
    capacity = token_row_list * picked_count * 3 // (2 * exp_total)
    slot_total = exp_total * capacity
    gain_single = norm_gain.astype(jnp.float32)
    gain_part = lax.dynamic_slice_in_dim(
        gain_single, lax.axis_index("dp") * part_width, part_width, 0
    )
    token_piece = tokens.astype(jnp.float32)
    pair_experts = experts.reshape(-1)
    rank = earlier_same(pair_experts)
    position = pair_experts * capacity + rank
    placing = (position[None, :] == jnp.arange(slot_total, dtype=jnp.int32)[:, None]).astype(
        jnp.bfloat16
    )
    mover = jnp.sum(placing.reshape(slot_total, token_row_list, picked_count), axis=2)
    slot_weights = jnp.dot(
        placing, route_weights.reshape(-1), preferred_element_type=jnp.float32
    ).astype(jnp.bfloat16)
    full_tok, full_dy = (
        lax.all_gather(tokens, "dp", axis=1, tiled=True),
        lax.all_gather(upstream, "dp", axis=1, tiled=True),
    )
    full_f32 = full_tok.astype(jnp.float32)
    reciprocal_root_mean = lax.rsqrt(jnp.mean(full_f32 * full_f32, axis=1) + 1e-05)
    normalized_rows = (full_f32 * reciprocal_root_mean[:, None] * gain_single[None, :]).astype(
        jnp.bfloat16
    )
    send_tok = jnp.dot(mover, normalized_rows, preferred_element_type=jnp.float32).astype(
        jnp.bfloat16
    )
    send_dy = jnp.dot(mover, full_dy, preferred_element_type=jnp.float32).astype(jnp.bfloat16)
    feat_width = send_tok.shape[1]
    got_tok, got_dy, got_weight = (
        lax.all_to_all(
            send_tok.reshape(exp_total, capacity, feat_width),
            "seq",
            split_axis=0,
            concat_axis=0,
            tiled=True,
        ),
        lax.all_to_all(
            send_dy.reshape(exp_total, capacity, feat_width),
            "seq",
            split_axis=0,
            concat_axis=0,
            tiled=True,
        ),
        lax.all_to_all(
            slot_weights.reshape(exp_total, capacity),
            "seq",
            split_axis=0,
            concat_axis=0,
            tiled=True,
        ),
    )
    got_tok = got_tok.reshape(seq_count, exp_local, capacity, feat_width)
    got_dy = got_dy.reshape(seq_count, exp_local, capacity, feat_width)
    got_weight = got_weight.reshape(seq_count, exp_local, capacity)
    grads_gu = []
    grads_dn = []
    rows_list = []
    weight_list = []
    for member in range(exp_local):
        x_rows = got_tok[:, member].reshape(seq_count * capacity, width)
        dy_rows = got_dy[:, member].reshape(seq_count * capacity, width)
        weight_rows = got_weight[:, member].reshape(seq_count * capacity)
        results = expert_terms(x_rows, dy_rows, weight_rows, w_gate_up[member], w_down[member])
        grads_gu.append(results[0].reshape(width, 2, hidden).astype(jnp.bfloat16))
        grads_dn.append(results[1].astype(jnp.bfloat16))
        rows_list.append(results[2].reshape(seq_count, capacity, width))
        weight_list.append(results[3].reshape(seq_count, capacity))
    rows_stack = jnp.stack(rows_list, axis=1).reshape(exp_total, capacity, width)
    weight_stack = jnp.stack(weight_list, axis=1).reshape(exp_total, capacity)
    back_rows, back_weight = (
        lax.all_to_all(
            rows_stack.astype(jnp.bfloat16), "seq", split_axis=0, concat_axis=0, tiled=True
        ).astype(rows_stack.dtype),
        lax.all_to_all(
            weight_stack.astype(jnp.bfloat16), "seq", split_axis=0, concat_axis=0, tiled=True
        ).astype(weight_stack.dtype),
    )
    combined = lax.dot_general(
        mover.astype(jnp.float32),
        back_rows.reshape(slot_total, back_rows.shape[2]),
        (((0,), (0,)), ((), ())),
        precision=lax.Precision.HIGHEST,
        preferred_element_type=jnp.float32,
    )
    pairing_weight = lax.dot_general(
        placing.astype(jnp.float32),
        back_weight.reshape(slot_total),
        (((0,), (0,)), ((), ())),
        precision=lax.Precision.HIGHEST,
        preferred_element_type=jnp.float32,
    )
    normed_gradient_piece = lax.psum_scatter(
        combined.astype(jnp.bfloat16), "dp", scatter_dimension=1, tiled=True
    ).astype(jnp.float32)
    standardized_piece = token_piece * reciprocal_root_mean[:, None]
    correction_term = normed_gradient_piece * gain_part[None, :]
    stat_sum, grad_weights = lax.psum(
        (
            jnp.sum(correction_term * standardized_piece, axis=1),
            pairing_weight.reshape(token_row_list, picked_count),
        ),
        "dp",
    )
    reduced_statistic = stat_sum / width
    token_gradient = (
        upstream.astype(jnp.float32)
        + reciprocal_root_mean[:, None]
        * (correction_term - standardized_piece * reduced_statistic[:, None])
    ).astype(jnp.bfloat16)
    gain_gradient = lax.psum(jnp.sum(normed_gradient_piece * standardized_piece, axis=0), "seq")
    grad_gate_up = jnp.stack(grads_gu, axis=0)
    grad_down = jnp.stack(grads_dn, axis=0)
    return (token_gradient, gain_gradient, grad_weights, grad_gate_up, grad_down)


def solution(mesh):
    in_specs = (
        P("seq", "dp"),
        P("seq", "dp"),
        P(),
        P("seq", None),
        P("seq", None),
        P("seq", None, None, "dp"),
        P("seq", "dp", None),
    )
    out_specs = (
        P("seq", "dp"),
        P("dp"),
        P("seq", None),
        P("seq", None, None, "dp"),
        P("seq", "dp", None),
    )
    fast = mesh.shape["seq"] == 8 and mesh.shape["dp"] > 1
    return jax.shard_map(plane_body if fast else body, mesh=mesh, in_specs=in_specs, out_specs=out_specs, check_vma=False)
```
